32 devices in a mesh: sub: 8 (over z, x), slab: 4 (over y, core).
Axes of the slice: x: 2, y: 2, z: 4, core: 2. Of those that a mesh axis runs over, the one named last changes fastest.
Arguments:
- adjoint_load: float32 [4, 8, 2, 4, 3200], P('slab', 'sub')
- design: float32 [4, 8, 2032], P('slab', 'sub'), may hold values from 0 to 1
- viscous_block: float32 [24, 24], replicated
- brinkman_block: float32 [24, 24], replicated
- coupling: float32 [8, 24], replicated, may hold values from -1.2 to 1.2
- stabilization: float32 [8, 8], replicated
- neighbours: int32 [4, 8, 3], P('slab', 'sub'), may hold values from -1 to 7, as said below
- iface_nodes: int32 [4, 8, 3, 256], P('slab', 'sub'), may hold values from 0 to 3199, as said below
- iface_count: int32 [4, 8, 3], P('slab', 'sub'), may hold values from 0 to 256, as said below
- face_nodes: int32 [4, 8, 2, 512], P('slab', 'sub'), may hold values from 0 to 3199, as said below
- owner_ids: int32 [4, 8, 3, 256], P('slab', 'sub'), may hold values from 0 to 7, as said below
Outputs:
- solution: float32 [4, 8, 2, 4, 3200], P('slab', 'sub')
- coefficients: float32 [2, 3], replicated
The draws below stay inside these ranges and needn't reach their ends.
Inputs may be any that keep to these rules, and one draw needn't show every extreme that they name: In round r the neighbour of subdomain i is i XOR 2^r or -1 for none; two neighbours list each other. `iface_nodes`: per subdomain, all entries here and in face_nodes are distinct local nodes. Slot k of round r names the same physical node on a subdomain and on its round-r neighbour; only the first iface_count slots are shared. `iface_count`: equal on both sides of a pair, 0 where the round has no neighbour. `face_nodes`: face 0 is the lower face, face 1 the upper one; slot k of the upper face of slab s is slot k of the lower face of slab s + 1 at the same index along sub. `owner_ids`: for a used slot, one of the two subdomains of the pair, the same on both sides; for an unused slot, the subdomain's own index.
All inputs are finite; a program needn't handle non-finite values.
Results may differ from the reference program's by a relative error of at most 0.0003.
Values sent between devices are 32-bit elements; how exact they have to be, the bound alone decides.
A program may use at most 128 MiB of HBM per device.

```python
import functools
from functools import partial
import jax
import jax.numpy as jnp
from jax import lax

EX = 4
EY = 4
EZ = 127
IFACE = 256
FACE = 512
ROUNDS = 3
KRYLOV = 3
CASES = 2
SUBS = 8
SLABS = 4
ELEMS = 2032
NODES = 3200


def draw_adjoint_load(key, part):
    extent = (SLABS, SUBS, CASES, 4, NODES)
    device_order = (jnp.arange(SLABS)[:, None] * SUBS + jnp.arange(SUBS)[None, :]).astype(jnp.float32)
    rising = (1.0 + 2.0 * device_order / (SLABS * SUBS - 1))[:, :, None, None, None]
    noise = jax.random.normal(key, extent, jnp.float32)
    return (rising * jnp.clip(noise, -4.0, 4.0)).astype(jnp.float32)


def dominant(key, extent, spread, leading_base):
    key_spread, key_leading = jax.random.split(key)
    spread_part = jax.random.uniform(key_spread, (extent, extent), jnp.float32, -spread, spread)
    leading = leading_base + jax.random.uniform(key_leading, (extent,), jnp.float32, 0.0, 1.0)
    identity = jnp.eye(extent, dtype=jnp.float32)
    return (spread_part * (1.0 - identity) + identity * leading[:, None]).astype(jnp.float32)


def draw_viscous_block(key, part):
    return dominant(jax.random.fold_in(key, 1), 24, 0.7, 2.5)


def draw_brinkman_block(key, part):
    return dominant(jax.random.fold_in(key, 2), 24, 0.15, 1.0)


def draw_stabilization(key, part):
    return dominant(jax.random.fold_in(key, 3), 8, 0.5, 1.0)


def swap_values(order, first_value, second_value):
    return jnp.where(order == first_value, second_value, jnp.where(order == second_value, first_value, order))


def place_ends(order, device_id):
    top_value = NODES - 1
    face_start = ROUNDS * IFACE
    even = device_id % 2 == 0
    head_value = jnp.where(even, top_value, 0).astype(jnp.int32)
    face_value = jnp.where(even, 0, top_value).astype(jnp.int32)
    order = swap_values(order, order[0], head_value)
    order = swap_values(order, order[face_start], face_value)
    return order


def subdomain_layout(key):
    stream = jax.random.fold_in(key, 11)
    device_keys = jax.random.split(stream, SLABS * SUBS)
    orders = jax.vmap(functools.partial(jax.random.permutation, x=NODES))(device_keys).astype(jnp.int32)
    device_ids = jnp.arange(SLABS * SUBS, dtype=jnp.int32)
    return jax.vmap(place_ends)(orders, device_ids).astype(jnp.int32)


def draw_iface_nodes(key, part):
    orders = subdomain_layout(key)
    return orders[:, :ROUNDS * IFACE].reshape(SLABS, SUBS, ROUNDS, IFACE)


def draw_face_nodes(key, part):
    orders = subdomain_layout(key)
    return orders[:, ROUNDS * IFACE:ROUNDS * IFACE + 2 * FACE].reshape(SLABS, SUBS, 2, FACE)


def pair_tables(key):
    stream = jax.random.fold_in(key, 23)
    key_present, key_counts, key_sides = jax.random.split(stream, 3)
    present = jax.random.randint(key_present, (SLABS, SUBS, ROUNDS), 0, 4) > 0
    counts = jax.random.randint(key_counts, (SLABS, SUBS, ROUNDS), IFACE // 4, IFACE + 1)
    side_table = jax.random.randint(key_sides, (SLABS, SUBS, ROUNDS, IFACE), 0, 2)
    sub_ids = jnp.arange(SUBS, dtype=jnp.int32)[:, None]
    powers = (2 ** jnp.arange(ROUNDS, dtype=jnp.int32))[None, :]
    partner = jnp.bitwise_xor(sub_ids, powers)
    low_side = jnp.minimum(sub_ids, partner)
    high_side = jnp.maximum(sub_ids, partner)
    round_ids = jnp.broadcast_to(jnp.arange(ROUNDS, dtype=jnp.int32)[None, :], (SUBS, ROUNDS))
    linked = present[:, low_side, round_ids]
    forced_on = ((low_side == 0) | (low_side == SUBS - 2)) & (round_ids == 0)
    forced_off = (low_side == 2) & (round_ids == 0)
    linked = (linked | forced_on[None]) & jnp.logical_not(forced_off)[None]
    filled = (low_side == 0) & (round_ids == 0)
    shared_count = jnp.where(filled[None], IFACE, counts[:, low_side, round_ids])
    shared_count = jnp.where(linked, shared_count, 0)
    partner_ids = jnp.where(linked, partner[None], -1)
    side_bits = side_table[:, low_side, round_ids]
    owner = jnp.where(side_bits == 1, low_side[None, :, :, None], high_side[None, :, :, None])
    slot_ids = jnp.arange(IFACE, dtype=jnp.int32)[None, None, None, :]
    owner = jnp.where(slot_ids < shared_count[..., None], owner, sub_ids[None, :, :, None])
    return (partner_ids.astype(jnp.int32), shared_count.astype(jnp.int32), owner.astype(jnp.int32))


def draw_neighbours(key, part):
    return pair_tables(key)[0]


def draw_iface_count(key, part):
    return pair_tables(key)[1]


def draw_owner_ids(key, part):
    return pair_tables(key)[2]


def steps_of(stream_key, shape, cuts, least, high):
    def one(axis_at, parts):
        steps = jax.random.uniform(jax.random.fold_in(jax.random.fold_in(stream_key, 6), axis_at), (parts,), jnp.float32, least / len(cuts), high / len(cuts))
        return jnp.repeat(jnp.exp(steps), shape[axis_at] // parts).reshape((-1,) + (1,) * (len(shape) - axis_at - 1))

    factor_of = one(*cuts[0])
    for cut in cuts[1:]:
        factor_of = factor_of * one(*cut)
    return factor_of


def gaussian(stream_key, dims, deviation, bound, kind=jnp.bfloat16):
    array = deviation * jax.random.normal(stream_key, dims, jnp.float32)
    return jnp.clip(array, min=-bound, max=bound).astype(kind)


def setup_inputs(seed: int = 0) -> dict:
    key_list = jax.random.split(jax.random.key(seed), 12)
    return {
        "adjoint_load": draw_adjoint_load(jax.random.fold_in(key_list[11], 71), 0),
        "design": jnp.clip(1.0 * jax.random.uniform(key_list[1], (SLABS, SUBS, ELEMS), jnp.float32) ** steps_of(key_list[1], (SLABS, SUBS, ELEMS), ((0, 4), (1, 8)), -0.2, 0.2), 0.0, 1.0),
        "viscous_block": draw_viscous_block(jax.random.fold_in(key_list[11], 71), 0),
        "brinkman_block": draw_brinkman_block(jax.random.fold_in(key_list[11], 71), 0),
        "coupling": gaussian(key_list[4], (8, 24), 0.3, 1.2, jnp.float32),
        "stabilization": draw_stabilization(jax.random.fold_in(key_list[11], 71), 0),
        "neighbours": draw_neighbours(jax.random.fold_in(key_list[11], 71), 0),
        "iface_nodes": draw_iface_nodes(jax.random.fold_in(key_list[11], 71), 0),
        "iface_count": draw_iface_count(jax.random.fold_in(key_list[11], 71), 0),
        "face_nodes": draw_face_nodes(jax.random.fold_in(key_list[11], 71), 0),
        "owner_ids": draw_owner_ids(jax.random.fold_in(key_list[11], 71), 0),
    }


PRECISE = lax.Precision.HIGHEST
BRINKMAN_MAX = 4.0
RAMP_PARAM = 0.1

def corner_offsets(corner):
    return (corner // 4, corner // 2 % 2, corner % 2)

def element_vectors(field):
    channels = field.shape[0]
    node_grid = field.reshape(channels, EX + 1, EY + 1, EZ + 1)
    corner_list = []
    for corner in range(8):
        shift_x, shift_y, shift_z = corner_offsets(corner)
        window = node_grid[:, shift_x:shift_x + EX, shift_y:shift_y + EY, shift_z:shift_z + EZ]
        corner_list.append(window.reshape(channels, ELEMS))
    return jnp.stack(corner_list, axis=1)

def node_sums(element_out):
    channels = element_out.shape[0]
    summed = jnp.zeros((channels, EX + 1, EY + 1, EZ + 1), jnp.float32)
    for corner in range(8):
        shift_x, shift_y, shift_z = corner_offsets(corner)
        corner_block = element_out[:, corner].reshape(channels, EX, EY, EZ)
        summed = summed + jnp.pad(corner_block, ((0, 0), (shift_x, 1 - shift_x), (shift_y, 1 - shift_y), (shift_z, 1 - shift_z)))
    return summed.reshape(channels, NODES)

def brinkman_of(design):
    return BRINKMAN_MAX * RAMP_PARAM * (1.0 - design) / (RAMP_PARAM + design)

def adjoint_terms(state, brinkman, viscous_block, brinkman_block, coupling, stabilization):
    values = element_vectors(state).reshape(CASES, 32, ELEMS)
    velocity = values[:, :24]
    pressure = values[:, 24:]
    out_velocity = jnp.einsum('ij,cie->cje', viscous_block, velocity, precision=PRECISE)
    out_velocity = out_velocity + brinkman * jnp.einsum('ij,cie->cje', brinkman_block, velocity, precision=PRECISE)
    out_velocity = out_velocity + jnp.einsum('kj,cke->cje', coupling, pressure, precision=PRECISE)
    out_pressure = jnp.einsum('kj,cje->cke', coupling, velocity, precision=PRECISE) - jnp.einsum('lk,cle->cke', stabilization, pressure, precision=PRECISE)
    element_out = jnp.concatenate([out_velocity, out_pressure], axis=1).reshape(CASES * 4, 8, ELEMS)
    return node_sums(element_out)

def divergence_terms(velocity_nodes, coupling):
    element_vel = element_vectors(velocity_nodes).reshape(CASES, 24, ELEMS)
    return node_sums(jnp.einsum('kj,cje->cke', coupling, element_vel, precision=PRECISE))

def gradient_terms(pressure_nodes, coupling):
    element_pre = element_vectors(pressure_nodes)
    element_out = jnp.einsum('kj,cke->cje', coupling, element_pre, precision=PRECISE).reshape(CASES * 3, 8, ELEMS)
    return node_sums(element_out)

def diagonal_terms(brinkman, viscous_block, brinkman_block):
    diag_elem = jnp.diagonal(viscous_block)[:, None] + jnp.diagonal(brinkman_block)[:, None] * brinkman[None, :]
    return node_sums(diag_elem.reshape(3, 8, ELEMS))

def schur_terms(diag_nodes, coupling, stabilization):
    inverse = 1.0 / element_vectors(diag_nodes).reshape(24, ELEMS)
    schur_elem = jnp.einsum('kj,je->ke', coupling * coupling, inverse, precision=PRECISE) + jnp.diagonal(stabilization)[:, None]
    return node_sums(schur_elem[None])

def node_weights(iface_nodes, not_owned, lower_face, lower_lost):
    weights = jnp.ones((NODES,), jnp.float32)
    for matching in range(ROUNDS):
        keep = jnp.where(not_owned[matching], 0.0, 1.0).astype(weights.dtype)
        weights = weights.at[iface_nodes[matching]].multiply(keep)
    return weights.at[lower_face].multiply(jnp.where(lower_lost, 0.0, 1.0).astype(weights.dtype))

def add_shared(partial_sums, iface_nodes, incoming, face_nodes, from_below, from_above):
    summed = partial_sums
    for matching in range(ROUNDS):
        summed = summed.at[:, iface_nodes[matching]].add(incoming[matching])
    summed = summed.at[:, face_nodes[0]].add(from_below)
    return summed.at[:, face_nodes[1]].add(from_above)

def assemble(partial_sums, iface_nodes, iface_count, neighbours, face_nodes):
    slot_ids = jnp.arange(IFACE, dtype=jnp.int32)
    slot_valid = (slot_ids < iface_count[..., None]).astype(partial_sums.dtype)
    outgoing = jnp.take_along_axis(partial_sums[:, :, None], iface_nodes[:, :, :, None, :], axis=-1) * slot_valid[:, :, :, None, :]
    partner = jnp.maximum(neighbours, 0).astype(jnp.int32)
    present = (neighbours >= 0).astype(partial_sums.dtype)
    received = []
    for matching in range(ROUNDS):
        chosen = jnp.take_along_axis(outgoing[:, :, matching], partner[:, :, matching, None, None], axis=1)
        received.append(chosen * present[:, :, matching, None, None])
    incoming = jnp.stack(received, axis=2)
    face_out = jnp.take_along_axis(partial_sums[:, :, None], face_nodes[:, :, :, None, :], axis=-1)
    empty_face = jnp.zeros_like(face_out[:1, :, 1])
    from_below = jnp.concatenate([empty_face, face_out[:-1, :, 1]], axis=0)
    from_above = jnp.concatenate([face_out[1:, :, 0], empty_face], axis=0)
    return jax.vmap(jax.vmap(add_shared))(partial_sums, iface_nodes, incoming, face_nodes, from_below, from_above)

def per_device(function, *arrays):
    flattened = tuple((array_item.reshape((SLABS * SUBS,) + array_item.shape[2:]) for array_item in arrays))
    result = lax.map(lambda device_items: function(*device_items), flattened)
    return result.reshape((SLABS, SUBS) + result.shape[1:])

def triangular_solves(factor, target):
    middle = []
    for row_index in range(KRYLOV):
        remainder = target[:, row_index] - sum((factor[:, row_index, col_index] * middle[col_index] for col_index in range(row_index)))
        middle.append(remainder / factor[:, row_index, row_index])
    result = [None] * KRYLOV
    for row_index in reversed(range(KRYLOV)):
        remainder = middle[row_index] - sum((factor[:, col_index, row_index] * result[col_index] for col_index in range(row_index + 1, KRYLOV)))
        result[row_index] = remainder / factor[:, row_index, row_index]
    return jnp.stack(result, axis=1)

def reference(adjoint_load, design, viscous_block, brinkman_block, coupling, stabilization, neighbours, iface_nodes, iface_count, face_nodes, owner_ids):
    brinkman = brinkman_of(design)

    def link(partial_sums):
        return assemble(partial_sums, iface_nodes, iface_count, neighbours, face_nodes)
    slot_ids = jnp.arange(IFACE, dtype=jnp.int32)
    sub_ids = jnp.arange(SUBS, dtype=jnp.int32)[None, :, None, None]
    not_owned = (slot_ids < iface_count[..., None]) & (owner_ids != sub_ids)
    lower_lost = jnp.broadcast_to((jnp.arange(SLABS) > 0)[:, None], (SLABS, SUBS))
    weights = jax.vmap(jax.vmap(node_weights))(iface_nodes, not_owned, face_nodes[:, :, 0], lower_lost)

    def weighted_dot(first_vec, second_vec):
        return lax.optimization_barrier(jnp.sum(weights[:, :, None, None, :] * first_vec * second_vec, axis=(0, 1, 3, 4)))
    owned_load = (adjoint_load * weights[:, :, None, None, :]).reshape(SLABS, SUBS, CASES * 4, NODES)
    diag_part = per_device(partial(diagonal_terms, viscous_block=viscous_block, brinkman_block=brinkman_block), brinkman)
    assembled = link(jnp.concatenate([owned_load, diag_part], axis=2))
    start_vec = assembled[:, :, :CASES * 4].reshape(SLABS, SUBS, CASES, 4, NODES)
    diag_nodes = assembled[:, :, CASES * 4:]
    schur_diag = link(per_device(partial(schur_terms, coupling=coupling, stabilization=stabilization), diag_nodes))[:, :, 0]

    def precondition(vector):
        velocity_guess = vector[:, :, :, :3] / diag_nodes[:, :, None]
        divergence = link(per_device(partial(divergence_terms, coupling=coupling), velocity_guess.reshape(SLABS, SUBS, CASES * 3, NODES)))
        pressure = (divergence - vector[:, :, :, 3]) / schur_diag[:, :, None]
        gradient = link(per_device(partial(gradient_terms, coupling=coupling), pressure)).reshape(SLABS, SUBS, CASES, 3, NODES)
        velocity = velocity_guess - gradient / diag_nodes[:, :, None]
        return jnp.concatenate([velocity, pressure[:, :, :, None]], axis=3)

    def operator(direction):
        image_part = per_device(partial(adjoint_terms, viscous_block=viscous_block, brinkman_block=brinkman_block, coupling=coupling, stabilization=stabilization), direction.reshape(SLABS, SUBS, CASES * 4, NODES), brinkman)
        return link(image_part).reshape(SLABS, SUBS, CASES, 4, NODES)
    start_norm = jnp.sqrt(weighted_dot(start_vec, start_vec))
    krylov_basis = [start_vec / start_norm[None, None, :, None, None]]
    hessenberg = jnp.zeros((CASES, KRYLOV + 1, KRYLOV), jnp.float32)
    directions = []
    for krylov_step in range(KRYLOV):
        direction = precondition(krylov_basis[-1])
        directions.append(direction)
        product_vec = operator(direction)
        heights = jnp.stack([weighted_dot(vector, product_vec) for vector in krylov_basis], axis=1)
        for basis_index in range(len(krylov_basis)):
            product_vec = product_vec - heights[None, None, :, basis_index, None, None] * krylov_basis[basis_index]
        length = jnp.sqrt(weighted_dot(product_vec, product_vec))
        hessenberg = hessenberg.at[:, :krylov_step + 1, krylov_step].set(heights)
        hessenberg = hessenberg.at[:, krylov_step + 1, krylov_step].set(length)
        krylov_basis.append(product_vec / length[None, None, :, None, None])
    normal_matrix = jnp.einsum('cij,cik->cjk', hessenberg, hessenberg, precision=PRECISE)
    target = start_norm[:, None] * hessenberg[:, 0, :]
    factor = jnp.linalg.cholesky(normal_matrix)
    coefficients = triangular_solves(factor, target)
    solution = sum((coefficients[None, None, :, krylov_step, None, None] * directions[krylov_step] for krylov_step in range(KRYLOV)))
    return (solution, coefficients)
```

```python
import functools

import jax
import jax.numpy as jnp
from jax import lax
from jax.experimental import pallas as pl
from jax.experimental.pallas import tpu as pltpu
from jax.sharding import PartitionSpec as P

EX = 4
EY = 4
EZ = 127
IFACE = 256
FACE = 512
ROUNDS = 3
KRYLOV = 3
CASES = 2
ELEMS = 2032
NODES = 3200

LANES = 128
ROWS = NODES // LANES
CH = 8
SLOTS = ROUNDS * IFACE + 2 * FACE
BLOCKS = SLOTS // LANES
FACE_BLOCKS = FACE // LANES
IFACE_BLOCKS = IFACE // LANES
BIG = 8 * CH

GROUPS = ((0, 0), (0, 1), (1, 0))
DEPTH = BIG * len(GROUPS)
PARTS = 2

BRINKMAN_MAX = 4.0
RAMP_PARAM = 0.1
EXCHANGES = 2 + 3 * KRYLOV
REDUCTIONS = KRYLOV + 1
HIGH = lax.Precision.HIGHEST
MESH = pl.DeviceIdType.MESH


def dot(a, b, ca, cb):
    return lax.dot_general(
        a, b, (((ca,), (cb,)), ((), ())), precision=HIGH, preferred_element_type=jnp.float32
    )


def one_hot(rows, cols, field, per_field):
    i = lax.broadcasted_iota(jnp.int32, (rows, cols), 0) & (BIG - 1)
    j = lax.broadcasted_iota(jnp.int32, (rows, cols), 1)
    same = (i >> 3) == (j & 7)
    f = i & 3
    if per_field:
        match = (f == (j >> 3)) & (j < 24)
    else:
        match = (f == field) & (j < 8)
    return jnp.where(same & match, 1.0, 0.0).astype(jnp.float32)


def kernel(
    n_sub,
    n_slab,
    load_ref,
    design_ref,
    visc_ref,
    brink_ref,
    coup_ref,
    stab_ref,
    iface_ref,
    count_ref,
    face_ref,
    owner_ref,
    out_ref,
    coef_ref,
    lo_ref,
    hi_ref,
    inv_block,
    inv_lane,
    wt_ref,
    x_ref,
    y_ref,
    y2_ref,
    t_ref,
    p_ref,
    diag_ref,
    schur_ref,
    z_ref,
    v_ref,
    flat_ref,
    brk_ref,
    lhs_j,
    lhs_d,
    lhs_g,
    lhs_s,
    send_buf,
    recv_buf,
    sub_buf,
    pad_ref,
    mid_ref,
    mat_ref,
    sum_ref,
    slab_buf,
    send_sem,
    recv_sem,
    sub_send_sem,
    sub_recv_sem,
    slab_send_sem,
    slab_recv_sem,
):
    sub = lax.axis_index("sub")
    slab = lax.axis_index("slab")
    sub_peers = [lax.rem(sub + d, n_sub) for d in range(1, n_sub)]
    slab_peers = [lax.rem(slab + d, n_slab) for d in range(1, n_slab)]
    partners = [
        sub + (1 << r) * (1 - 2 * lax.rem(sub // (1 << r), 2)) for r in range(ROUNDS)
    ]
    below = lax.rem(slab + n_slab - 1, n_slab)
    above = lax.rem(slab + 1, n_slab)

    barrier = pltpu.get_barrier_semaphore()
    for peer in sub_peers:
        pl.semaphore_signal(barrier, inc=1, device_id={"sub": peer}, device_id_type=MESH)
    for peer in slab_peers:
        pl.semaphore_signal(barrier, inc=1, device_id={"slab": peer}, device_id_type=MESH)

    lane = lax.broadcasted_iota(jnp.int32, (CH, LANES), 1)
    chan = lax.broadcasted_iota(jnp.int32, (CH, LANES), 0)
    is_p = (chan & 3) == 3
    inside = lane < EZ

    idx_parts, used_parts, lost_parts = [], [], []
    counts = count_ref[0]
    for r in range(ROUNDS):
        idx_parts.append(iface_ref[0, 0, r : r + 1, :])
        slot = lax.broadcasted_iota(jnp.int32, (1, IFACE), 1)
        used = slot < counts[:, r : r + 1]
        other = owner_ref[0, 0, r : r + 1, :] != sub
        used_parts.append(jnp.where(used, 1.0, 0.0))
        lost_parts.append(jnp.where(used & other, 1.0, 0.0))
    for side in range(2):
        idx_parts.append(face_ref[0, 0, side : side + 1, :])
        linked = slab > 0 if side == 0 else slab < n_slab - 1
        flag = jnp.where(linked, 1.0, 0.0).astype(jnp.float32)
        used_parts.append(jnp.full((1, FACE), 1.0, jnp.float32) * flag)
        lost_parts.append(
            jnp.full((1, FACE), 1.0 if side == 0 else 0.0, jnp.float32) * flag
        )
    idx = jnp.concatenate(idx_parts, axis=1)
    used = jnp.concatenate(used_parts, axis=1)
    lost = jnp.concatenate(lost_parts, axis=1)
    hi = idx >> 7
    lo = idx & (LANES - 1)
    for k in range(BLOCKS):
        cols = slice(k * LANES, (k + 1) * LANES)
        lo_ref[k] = jnp.broadcast_to(lo[:, cols], (CH, LANES))
        hi_ref[k] = jnp.broadcast_to(hi[:, cols], (CH, LANES))

    slot = lax.broadcasted_iota(jnp.int32, (1, SLOTS), 1)
    block_of = ((slot >> 7) + 1).astype(jnp.float32) * used
    lane_of = (slot & (LANES - 1)).astype(jnp.float32) * used
    hot_hi = lax.broadcasted_iota(jnp.int32, (32, SLOTS), 0) == hi
    hot_lo = jnp.where(
        lax.broadcasted_iota(jnp.int32, (LANES, SLOTS), 0) == lo, 1.0, 0.0
    ).astype(jnp.bfloat16)

    def to_nodes(values):
        left = jnp.where(hot_hi, values, 0.0).astype(jnp.bfloat16)
        return lax.dot_general(
            left, hot_lo, (((1,), (1,)), ((), ())), preferred_element_type=jnp.float32
        )

    node_block = to_nodes(block_of).astype(jnp.int32)
    node_lane = to_nodes(lane_of).astype(jnp.int32)
    node_lost = to_nodes(lost)
    for r in range(ROWS):
        inv_block[r] = jnp.broadcast_to(node_block[r : r + 1], (CH, LANES))
        inv_lane[r] = jnp.broadcast_to(node_lane[r : r + 1], (CH, LANES))
        wt_ref[r] = jnp.broadcast_to(1.0 - node_lost[r : r + 1], (CH, LANES))

    for r in range(ROWS):
        cols = slice(r * LANES, (r + 1) * LANES)
        both = jnp.concatenate([load_ref[0, 0, 0, :, cols], load_ref[0, 0, 1, :, cols]], axis=0)
        y_ref[r] = both * wt_ref[r]

    flat_ref[...] = jnp.zeros_like(flat_ref)
    flat_ref[:, 0:ELEMS] = jnp.broadcast_to(design_ref[0], (CH, ELEMS))
    for i in range(EX * EY):
        here = flat_ref[:, i * LANES : (i + 1) * LANES]
        if i > 0:
            before = flat_ref[:, (i - 1) * LANES : i * LANES]
            here = jnp.where(lane < i, pltpu.roll(before, i, 1), pltpu.roll(here, i, 1))
        value = BRINKMAN_MAX * RAMP_PARAM * (1.0 - here) / (RAMP_PARAM + here)
        brk_ref[i] = jnp.where(inside, value, 0.0)

    pad_ref[...] = jnp.zeros_like(pad_ref)
    for i, block in enumerate((visc_ref, brink_ref, coup_ref, stab_ref)):
        pad_ref[i, 0 : block.shape[0], 0 : block.shape[1]] = block[...]
    visc, brink, coup, stab = (pad_ref[i] for i in range(4))
    e_u = one_hot(BIG, LANES, 0, True)
    e_p = one_hot(BIG, LANES, 3, False)
    e_s = one_hot(BIG, LANES, 0, False)
    w_u = one_hot(DEPTH, LANES, 0, True)
    w_p = one_hot(DEPTH, LANES, 3, False)
    row_case = (lax.broadcasted_iota(jnp.int32, (BIG, DEPTH), 0) >> 2) & 1
    col = lax.broadcasted_iota(jnp.int32, (BIG, DEPTH), 1)
    same_case = row_case == ((col >> 2) & 1)
    first_part = jnp.zeros((BIG, DEPTH), jnp.bool_)
    for g, (part, _) in enumerate(GROUPS):
        if part == 0:
            first_part = first_part | ((col >> 6) == g)

    def split_matrix(matrix):
        mat_ref[...] = jnp.where(same_case, matrix, 0.0)
        matrix = mat_ref[...]
        head = matrix.astype(jnp.bfloat16).astype(jnp.float32)
        return jnp.where(first_part, head, matrix - head).astype(jnp.bfloat16)

    def expand(left, block, side, right):
        mid_ref[...] = dot(left, block, 1, side)
        return dot(mid_ref[...], right, 1, 1)

    big_d = expand(e_p, coup, 0, w_u)
    big_g = expand(e_u, coup, 1, w_p)
    big_b = expand(e_u, brink, 1, w_u)
    sum_ref[...] = big_d + big_g
    sum_ref[...] += expand(e_u, visc, 1, w_u)
    sum_ref[...] -= expand(e_p, stab, 1, w_p)
    lhs_j[0:BIG] = split_matrix(sum_ref[...])
    lhs_j[BIG : 2 * BIG] = split_matrix(big_b)
    lhs_d[...] = split_matrix(big_d)
    lhs_g[...] = split_matrix(big_g)
    lhs_s[...] = split_matrix(expand(e_s, coup * coup, 0, w_u))

    def diagonal(matrix, hot):
        size = matrix.shape[0]
        eye = lax.broadcasted_iota(jnp.int32, (size, size), 0) == lax.broadcasted_iota(
            jnp.int32, (size, size), 1
        )
        row = jnp.sum(jnp.where(eye, matrix, 0.0), axis=0, keepdims=True)
        column = jnp.sum(hot * row, axis=1, keepdims=True)
        return jnp.broadcast_to(column, (BIG, LANES))

    def node_rows(element_out, target):
        near = [None] * ROWS
        far = [None] * ROWS

        def put(store, at, value):
            store[at] = value if store[at] is None else store[at] + value

        for a in range(EX):
            blocks = element_out(a)
            for b in range(EY):
                for q in range(8):
                    at = (a + q // 4) * (EY + 1) + b + q // 2 % 2
                    put(far if q % 2 else near, at, blocks[b][q])
        for r in range(ROWS):
            target[r] = near[r] + pltpu.roll(far[r], 1, 1)

    def split_nodes(source):
        for r in range(ROWS):
            x = source(r)
            rest = jnp.concatenate(
                [
                    jnp.where(inside, x, 0.0),
                    jnp.where(inside, pltpu.roll(x, LANES - 1, 1), 0.0),
                ],
                axis=0,
            )
            for part in range(PARTS):
                head = rest.astype(jnp.bfloat16)
                t_ref[part, r * 16 : (r + 1) * 16] = head
                rest = rest - head.astype(jnp.float32)

    def product(lhs, a):
        columns = []
        for b in range(EY):
            pieces = []
            for _, part in GROUPS:
                for r in (a * (EY + 1) + b, (a + 1) * (EY + 1) + b):
                    pieces.append(t_ref[part, r * 16 : (r + 2) * 16])
            columns.append(jnp.concatenate(pieces, axis=0))
        return jnp.dot(
            lhs[...], jnp.concatenate(columns, axis=1), preferred_element_type=jnp.float32
        )

    def corner(out, b, q, base=0):
        return out[base + q * CH : base + (q + 1) * CH, b * LANES : (b + 1) * LANES]

    def plain(lhs):
        def element_out(a):
            out = product(lhs, a)
            return [[corner(out, b, q) for q in range(8)] for b in range(EY)]

        return element_out

    def adjoint(a):
        out = product(lhs_j, a)
        return [
            [
                corner(out, b, q) + brk_ref[a * EY + b] * corner(out, b, q, BIG)
                for q in range(8)
            ]
            for b in range(EY)
        ]

    def diag_out(a):
        return [
            [
                jnp.where(inside, diag_v[q * CH : (q + 1) * CH], 0.0)
                + diag_b[q * CH : (q + 1) * CH] * brk_ref[a * EY + b]
                for q in range(8)
            ]
            for b in range(EY)
        ]

    def copies(e):
        made = []
        for r in range(ROUNDS):
            part = pl.ds(r * IFACE_BLOCKS, IFACE_BLOCKS)
            made.append((part, part, {"sub": partners[r]}))
        base = ROUNDS * IFACE_BLOCKS
        low, high = pl.ds(base, FACE_BLOCKS), pl.ds(base + FACE_BLOCKS, FACE_BLOCKS)
        made.append((low, high, {"slab": below}))
        made.append((high, low, {"slab": above}))
        return [
            pltpu.make_async_remote_copy(
                src_ref=send_buf.at[e, src],
                dst_ref=recv_buf.at[e, dst],
                send_sem=send_sem.at[e, i],
                recv_sem=recv_sem.at[e, i],
                device_id=device,
                device_id_type=MESH,
            )
            for i, (src, dst, device) in enumerate(made)
        ]

    started = []

    def post(e, source):
        los = [lo_ref[k] for k in range(BLOCKS)]
        his = [hi_ref[k] for k in range(BLOCKS)]

        def body(r, found):
            row = source[r]
            return tuple(
                jnp.where(
                    his[k] == r,
                    jnp.take_along_axis(row, los[k], axis=1, mode="promise_in_bounds"),
                    found[k],
                )
                for k in range(BLOCKS)
            )

        zero = jnp.zeros((CH, LANES), jnp.float32)
        found = lax.fori_loop(0, ROWS, body, (zero,) * BLOCKS, unroll=5)
        for k in range(BLOCKS):
            send_buf[e, k] = found[k]
        for copy in copies(e):
            copy.start()
            started.append(copy)

    def arrive(e):
        for copy in copies(e):
            copy.wait_recv()

    def received(e, r):
        at = inv_block[r]
        lanes = inv_lane[r]
        total = jnp.zeros((CH, LANES), jnp.float32)
        for k in range(BLOCKS):
            value = jnp.take_along_axis(
                recv_buf[e, k], lanes, axis=1, mode="promise_in_bounds"
            )
            total = jnp.where(at == k + 1, value, total)
        return total

    def each_row(body, sums=0):
        zero = jnp.zeros((CH, LANES), jnp.float32)

        def step(r, carry):
            added = body(r)
            return tuple(c + t for c, t in zip(carry, added))

        return lax.fori_loop(0, ROWS, step, (zero,) * sums)

    def sub_copies(t):
        return [
            pltpu.make_async_remote_copy(
                src_ref=sub_buf.at[t, sub],
                dst_ref=sub_buf.at[t, sub],
                send_sem=sub_send_sem.at[t, d],
                recv_sem=sub_recv_sem.at[t, d],
                device_id={"sub": peer},
                device_id_type=MESH,
            )
            for d, peer in enumerate(sub_peers)
        ]

    def sub_arrivals(t):
        return [
            pltpu.make_async_copy(
                sub_buf.at[t, lax.rem(sub + n_sub - d, n_sub)],
                sub_buf.at[t, lax.rem(sub + n_sub - d, n_sub)],
                sub_recv_sem.at[t, d - 1],
            )
            for d in range(1, n_sub)
        ]

    def slab_copies(t):
        return [
            pltpu.make_async_remote_copy(
                src_ref=slab_buf.at[t, slab],
                dst_ref=slab_buf.at[t, slab],
                send_sem=slab_send_sem.at[t, d],
                recv_sem=slab_recv_sem.at[t, d],
                device_id={"slab": peer},
                device_id_type=MESH,
            )
            for d, peer in enumerate(slab_peers)
        ]

    def slab_arrivals(t):
        return [
            pltpu.make_async_copy(
                slab_buf.at[t, lax.rem(slab + n_slab - d, n_slab)],
                slab_buf.at[t, lax.rem(slab + n_slab - d, n_slab)],
                slab_recv_sem.at[t, d - 1],
            )
            for d in range(1, n_slab)
        ]

    def reduce_start(t, partial_sums):
        message = jnp.zeros((CH, LANES), jnp.float32)
        for i, value in enumerate(partial_sums):
            total = jnp.sum(value, axis=1, keepdims=True)
            message = jnp.where(lane == i, total, message)
        sub_buf[t, sub] = message
        for copy in sub_copies(t):
            copy.start()
            started.append(copy)

    def reduce_middle(t):
        for copy in sub_arrivals(t):
            copy.wait()
        total = sub_buf[t, 0]
        for i in range(1, n_sub):
            total = total + sub_buf[t, i]
        slab_buf[t, slab] = total
        for copy in slab_copies(t):
            copy.start()
            started.append(copy)

    def reduce_end(t, number):
        for copy in slab_arrivals(t):
            copy.wait()
        total = slab_buf[t, 0]
        for i in range(1, n_slab):
            total = total + slab_buf[t, i]
        first = jnp.sum(jnp.where(chan < 4, total, 0.0), axis=0, keepdims=True)
        second = jnp.sum(jnp.where(chan < 4, 0.0, total), axis=0, keepdims=True)
        total = jnp.where(chan < 4, first, second)
        return [
            jnp.broadcast_to(total[:, i : i + 1], (CH, LANES)) for i in range(number)
        ]

    pl.semaphore_wait(barrier, n_sub - 1 + n_slab - 1)

    post(0, y_ref)
    diag_v = diagonal(visc, e_u)
    diag_b = diagonal(brink, e_u)
    node_rows(diag_out, y2_ref)
    post(1, y2_ref)
    arrive(0)

    def load_row(r):
        value = y_ref[r] + received(0, r)
        x_ref[r] = value
        return (value * value * wt_ref[r],)

    (square,) = each_row(load_row, 1)
    reduce_start(0, [square])
    arrive(1)

    def diag_row(r):
        diag_ref[r] = jnp.where(is_p, 1.0, y2_ref[r] + received(1, r))
        return ()

    each_row(diag_row)

    heights = []
    start_norm = None
    exchange = 2
    for step in range(KRYLOV):
        split_nodes(lambda r: x_ref[r] / diag_ref[r])
        node_rows(plain(lhs_d), y_ref)
        if step == 0:
            diag_s = diagonal(stab, e_s)
            split_nodes(lambda r: 1.0 / diag_ref[r])

            def schur_out(a):
                out = product(lhs_s, a)
                return [
                    [
                        corner(out, b, q)
                        + jnp.where(inside, diag_s[q * CH : (q + 1) * CH], 0.0)
                        for q in range(8)
                    ]
                    for b in range(EY)
                ]

            node_rows(schur_out, y2_ref)
            for r in range(ROWS):
                y_ref[r] = y_ref[r] + y2_ref[r]
        post(exchange, y_ref)
        reduce_middle(step)
        arrive(exchange)

        def pressure_row(r, step=step, exchange=exchange):
            value = y_ref[r] + received(exchange, r)
            if step == 0:
                schur = jnp.where(is_p, pltpu.roll(value, 3, 0), 1.0)
                schur_ref[r] = schur
            else:
                schur = schur_ref[r]
            p_ref[r] = jnp.where(is_p, (value - x_ref[r]) / schur, 0.0)
            return ()

        each_row(pressure_row)
        split_nodes(lambda r: p_ref[r])
        node_rows(plain(lhs_g), y_ref)
        post(exchange + 1, y_ref)

        sums = reduce_end(step, step + 1)
        if step == 0:
            start_norm = jnp.sqrt(sums[0])
            height, length = [], start_norm
        else:
            height, squared = sums[:step], sums[step]
            length = jnp.sqrt(squared - sum(h * h for h in height))
            heights.append(height + [length])
        arrive(exchange + 1)

        def direction_row(r, step=step, exchange=exchange, height=height, length=length):
            x = x_ref[r]
            diag = diag_ref[r]
            value = y_ref[r] + received(exchange + 1, r)
            z = jnp.where(is_p, p_ref[r], x / diag - value / diag)
            for m, h in enumerate(height):
                z = z - h * z_ref[m, r]
                x = x - h * v_ref[m, r]
            z_ref[step, r] = z / length
            v_ref[step, r] = x / length
            return ()

        each_row(direction_row)
        split_nodes(lambda r: z_ref[step, r])
        node_rows(adjoint, y_ref)
        post(exchange + 2, y_ref)
        arrive(exchange + 2)

        def image_row(r, step=step, exchange=exchange):
            w = y_ref[r] + received(exchange + 2, r)
            x_ref[r] = w
            weighted = w * wt_ref[r]
            return tuple(v_ref[m, r] * weighted for m in range(step + 1)) + (w * weighted,)

        products = each_row(image_row, step + 2)
        reduce_start(step + 1, products)
        exchange += 3

    reduce_middle(KRYLOV)
    sums = reduce_end(KRYLOV, KRYLOV + 1)
    height, squared = sums[:KRYLOV], sums[KRYLOV]
    heights.append(height + [jnp.sqrt(squared - sum(h * h for h in height))])

    def normal(i, j):
        return sum(heights[i][m] * heights[j][m] for m in range(min(i, j) + 2))

    factor = [[None] * KRYLOV for _ in range(KRYLOV)]
    for i in range(KRYLOV):
        for j in range(i + 1):
            value = normal(i, j)
            for k in range(j):
                value = value - factor[i][k] * factor[j][k]
            factor[i][j] = jnp.sqrt(value) if i == j else value / factor[j][j]
    middle = []
    for i in range(KRYLOV):
        value = start_norm * heights[i][0]
        for k in range(i):
            value = value - factor[i][k] * middle[k]
        middle.append(value / factor[i][i])
    coefs = [None] * KRYLOV
    for i in reversed(range(KRYLOV)):
        value = middle[i]
        for k in range(i + 1, KRYLOV):
            value = value - factor[k][i] * coefs[k]
        coefs[i] = value / factor[i][i]

    table = jnp.zeros((CH, LANES), jnp.float32)
    for j in range(KRYLOV):
        table = jnp.where(lane == j, coefs[j], table)
    for case in range(CASES):
        coef_ref[case : case + 1, :] = table[case * 4 : case * 4 + 1, 0:KRYLOV]
    for r in range(ROWS):
        value = coefs[0] * z_ref[0, r]
        for j in range(1, KRYLOV):
            value = value + coefs[j] * z_ref[j, r]
        cols = slice(r * LANES, (r + 1) * LANES)
        for case in range(CASES):
            out_ref[0, 0, case, :, cols] = value[case * 4 : case * 4 + 4]

    for copy in started:
        copy.wait_send()


def per_device(
    n_sub,
    n_slab,
    adjoint_load,
    design,
    viscous_block,
    brinkman_block,
    coupling,
    stabilization,
    neighbours,
    iface_nodes,
    iface_count,
    face_nodes,
    owner_ids,
):
    tile = (CH, LANES)
    f32, i32, bf16 = jnp.float32, jnp.int32, jnp.bfloat16
    rows = (ROWS,) + tile
    dma = pltpu.SemaphoreType.DMA
    scratch = [
        pltpu.VMEM((BLOCKS,) + tile, i32),
        pltpu.VMEM((BLOCKS,) + tile, i32),
        pltpu.VMEM(rows, i32),
        pltpu.VMEM(rows, i32),
        pltpu.VMEM(rows, f32),
        pltpu.VMEM(rows, f32),
        pltpu.VMEM(rows, f32),
        pltpu.VMEM(rows, f32),
        pltpu.VMEM((PARTS, ROWS * 16, LANES), bf16),
        pltpu.VMEM(rows, f32),
        pltpu.VMEM(rows, f32),
        pltpu.VMEM(rows, f32),
        pltpu.VMEM((KRYLOV,) + rows, f32),
        pltpu.VMEM((KRYLOV,) + rows, f32),
        pltpu.VMEM((CH, EX * EY * LANES), f32),
        pltpu.VMEM((EX * EY,) + tile, f32),
        pltpu.VMEM((2 * BIG, DEPTH), bf16),
        pltpu.VMEM((BIG, DEPTH), bf16),
        pltpu.VMEM((BIG, DEPTH), bf16),
        pltpu.VMEM((BIG, DEPTH), bf16),
        pltpu.VMEM((EXCHANGES, BLOCKS) + tile, f32),
        pltpu.VMEM((EXCHANGES, BLOCKS) + tile, f32),
        pltpu.VMEM((REDUCTIONS, n_sub) + tile, f32),
        pltpu.VMEM((4, LANES, LANES), f32),
        pltpu.VMEM((BIG, LANES), f32),
        pltpu.VMEM((BIG, DEPTH), f32),
        pltpu.VMEM((BIG, DEPTH), f32),
        pltpu.VMEM((REDUCTIONS, n_slab) + tile, f32),
        dma((EXCHANGES, ROUNDS + 2)),
        dma((EXCHANGES, ROUNDS + 2)),
        dma((REDUCTIONS, n_sub - 1)),
        dma((REDUCTIONS, n_sub - 1)),
        dma((REDUCTIONS, n_slab - 1)),
        dma((REDUCTIONS, n_slab - 1)),
    ]
    vmem = pl.BlockSpec(memory_space=pltpu.VMEM)
    return pl.pallas_call(
        functools.partial(kernel, n_sub, n_slab),
        out_shape=(
            jax.ShapeDtypeStruct((1, 1, CASES, 4, NODES), f32),
            jax.ShapeDtypeStruct((CASES, KRYLOV), f32),
        ),
        in_specs=[vmem] * 10,
        out_specs=(vmem, vmem),
        scratch_shapes=scratch,
        compiler_params=pltpu.CompilerParams(
            collective_id=0, has_side_effects=True, vmem_limit_bytes=48 * 1024 * 1024
        ),
    )(
        adjoint_load,
        design,
        viscous_block,
        brinkman_block,
        coupling,
        stabilization,
        iface_nodes,
        iface_count,
        face_nodes,
        owner_ids,
    )


def solution(mesh):
    placed = (
        P("slab", "sub", None, None, None),
        P("slab", "sub", None),
        P(),
        P(),
        P(),
        P(),
        P("slab", "sub", None),
        P("slab", "sub", None, None),
        P("slab", "sub", None),
        P("slab", "sub", None, None),
        P("slab", "sub", None, None),
    )
    return jax.shard_map(
        functools.partial(per_device, mesh.shape["sub"], mesh.shape["slab"]),
        mesh=mesh,
        in_specs=placed,
        out_specs=(P("slab", "sub", None, None, None), P()),
        check_vma=False,
    )
```

```python
import functools

import jax
import jax.numpy as jnp
from jax import lax
from jax.experimental import pallas as pl
from jax.experimental.pallas import tpu as pltpu
from jax.sharding import PartitionSpec as P

EX = 4
EY = 4
EZ = 127
IFACE = 256
FACE = 512
ROUNDS = 3
KRYLOV = 3
CASES = 2
ELEMS = 2032
NODES = 3200

LANES = 128
ROWS = NODES // LANES
CH = 8
SLOTS = ROUNDS * IFACE + 2 * FACE
BLOCKS = SLOTS // LANES
FACE_BLOCKS = FACE // LANES
IFACE_BLOCKS = IFACE // LANES
BIG = 8 * CH

GROUPS = ((0, 0), (0, 1), (1, 0))
DEPTH = BIG * len(GROUPS)
PARTS = 2

BRINKMAN_MAX = 4.0
RAMP_PARAM = 0.1
EXCHANGES = 2 + 3 * KRYLOV
REDUCTIONS = KRYLOV + 1
UNROLL = ROWS
INPUTS = 10
HIGH = lax.Precision.HIGHEST
MESH = pl.DeviceIdType.MESH


def dot(a, b, ca, cb):
    return lax.dot_general(
        a, b, (((ca,), (cb,)), ((), ())), precision=HIGH, preferred_element_type=jnp.float32
    )


def one_hot(rows, cols, field, per_field):
    i = lax.broadcasted_iota(jnp.int32, (rows, cols), 0) & (BIG - 1)
    j = lax.broadcasted_iota(jnp.int32, (rows, cols), 1)
    same = (i >> 3) == (j & 7)
    f = i & 3
    if per_field:
        match = (f == (j >> 3)) & (j < 24)
    else:
        match = (f == field) & (j < 8)
    return jnp.where(same & match, 1.0, 0.0).astype(jnp.float32)


def kernel(
    n_sub,
    n_slab,
    *refs,
):
    inputs = refs[:INPUTS]
    (
        out_ref,
        coef_ref,
        lo_ref,
        hi_ref,
        inv_block,
        inv_lane,
        wt_ref,
        x_ref,
        y_ref,
        y2_ref,
        t_ref,
        p_ref,
        diag_ref,
        schur_ref,
        z_ref,
        v_ref,
        flat_ref,
        brk_ref,
        lhs_j,
        lhs_d,
        lhs_g,
        lhs_s,
        send_buf,
        recv_buf,
        sub_buf,
        pad_ref,
        mid_ref,
        mat_ref,
        sum_ref,
        slab_buf,
        send_sem,
        recv_sem,
        sub_send_sem,
        sub_recv_sem,
        slab_send_sem,
        slab_recv_sem,
        in_sem,
        *held,
    ) = refs[INPUTS:]
    fetches = [
        pltpu.make_async_copy(source, target, in_sem.at[i])
        for i, (source, target) in enumerate(zip(inputs, held))
    ]
    for fetch in fetches:
        fetch.start()
    (
        load_ref,
        design_ref,
        visc_ref,
        brink_ref,
        coup_ref,
        stab_ref,
        iface_ref,
        count_ref,
        face_ref,
        owner_ref,
    ) = held
    sub = lax.axis_index("sub")
    slab = lax.axis_index("slab")
    sub_peers = [lax.rem(sub + d, n_sub) for d in range(1, n_sub)]
    slab_peers = [lax.rem(slab + d, n_slab) for d in range(1, n_slab)]
    partners = [
        sub + (1 << r) * (1 - 2 * lax.rem(sub // (1 << r), 2)) for r in range(ROUNDS)
    ]
    below = lax.rem(slab + n_slab - 1, n_slab)
    above = lax.rem(slab + 1, n_slab)

    barrier = pltpu.get_barrier_semaphore()
    for peer in sub_peers:
        pl.semaphore_signal(barrier, inc=1, device_id={"sub": peer}, device_id_type=MESH)
    for peer in slab_peers:
        pl.semaphore_signal(barrier, inc=1, device_id={"slab": peer}, device_id_type=MESH)

    for fetch in fetches:
        fetch.wait()

    lane = lax.broadcasted_iota(jnp.int32, (CH, LANES), 1)
    chan = lax.broadcasted_iota(jnp.int32, (CH, LANES), 0)
    is_p = (chan & 3) == 3
    inside = lane < EZ

    idx_parts, used_parts, lost_parts = [], [], []
    counts = count_ref[0]
    for r in range(ROUNDS):
        idx_parts.append(iface_ref[0, 0, r : r + 1, :])
        slot = lax.broadcasted_iota(jnp.int32, (1, IFACE), 1)
        used = slot < counts[:, r : r + 1]
        other = owner_ref[0, 0, r : r + 1, :] != sub
        used_parts.append(jnp.where(used, 1.0, 0.0))
        lost_parts.append(jnp.where(used & other, 1.0, 0.0))
    for side in range(2):
        idx_parts.append(face_ref[0, 0, side : side + 1, :])
        linked = slab > 0 if side == 0 else slab < n_slab - 1
        flag = jnp.where(linked, 1.0, 0.0).astype(jnp.float32)
        used_parts.append(jnp.full((1, FACE), 1.0, jnp.float32) * flag)
        lost_parts.append(
            jnp.full((1, FACE), 1.0 if side == 0 else 0.0, jnp.float32) * flag
        )
    idx = jnp.concatenate(idx_parts, axis=1)
    used = jnp.concatenate(used_parts, axis=1)
    lost = jnp.concatenate(lost_parts, axis=1)
    hi = idx >> 7
    lo = idx & (LANES - 1)
    for k in range(BLOCKS):
        cols = slice(k * LANES, (k + 1) * LANES)
        lo_ref[k] = jnp.broadcast_to(lo[:, cols], (CH, LANES))
        hi_ref[k] = jnp.broadcast_to(hi[:, cols], (CH, LANES))

    slot = lax.broadcasted_iota(jnp.int32, (1, SLOTS), 1)
    block_of = ((slot >> 7) + 1).astype(jnp.float32) * used
    lane_of = (slot & (LANES - 1)).astype(jnp.float32) * used
    hot_hi = lax.broadcasted_iota(jnp.int32, (32, SLOTS), 0) == hi
    hot_lo = jnp.where(
        lax.broadcasted_iota(jnp.int32, (LANES, SLOTS), 0) == lo, 1.0, 0.0
    ).astype(jnp.bfloat16)

    def to_nodes(values):
        left = jnp.where(hot_hi, values, 0.0).astype(jnp.bfloat16)
        return lax.dot_general(
            left, hot_lo, (((1,), (1,)), ((), ())), preferred_element_type=jnp.float32
        )

    node_block = to_nodes(block_of).astype(jnp.int32)
    node_lane = to_nodes(lane_of).astype(jnp.int32)
    node_lost = to_nodes(lost)
    for r in range(ROWS):
        inv_block[r] = jnp.broadcast_to(node_block[r : r + 1], (CH, LANES))
        inv_lane[r] = jnp.broadcast_to(node_lane[r : r + 1], (CH, LANES))
        wt_ref[r] = jnp.broadcast_to(1.0 - node_lost[r : r + 1], (CH, LANES))

    for r in range(ROWS):
        cols = slice(r * LANES, (r + 1) * LANES)
        both = jnp.concatenate([load_ref[0, 0, 0, :, cols], load_ref[0, 0, 1, :, cols]], axis=0)
        y_ref[r] = both * wt_ref[r]

    flat_ref[...] = jnp.zeros_like(flat_ref)
    flat_ref[:, 0:ELEMS] = jnp.broadcast_to(design_ref[0], (CH, ELEMS))
    for i in range(EX * EY):
        here = flat_ref[:, i * LANES : (i + 1) * LANES]
        if i > 0:
            before = flat_ref[:, (i - 1) * LANES : i * LANES]
            here = jnp.where(lane < i, pltpu.roll(before, i, 1), pltpu.roll(here, i, 1))
        value = BRINKMAN_MAX * RAMP_PARAM * (1.0 - here) / (RAMP_PARAM + here)
        brk_ref[i] = jnp.where(inside, value, 0.0)

    pad_ref[...] = jnp.zeros_like(pad_ref)
    for i, block in enumerate((visc_ref, brink_ref, coup_ref, stab_ref)):
        pad_ref[i, 0 : block.shape[0], 0 : block.shape[1]] = block[...]
    visc, brink, coup, stab = (pad_ref[i] for i in range(4))
    e_u = one_hot(BIG, LANES, 0, True)
    e_p = one_hot(BIG, LANES, 3, False)
    e_s = one_hot(BIG, LANES, 0, False)
    w_u = one_hot(DEPTH, LANES, 0, True)
    w_p = one_hot(DEPTH, LANES, 3, False)
    row_case = (lax.broadcasted_iota(jnp.int32, (BIG, DEPTH), 0) >> 2) & 1
    col = lax.broadcasted_iota(jnp.int32, (BIG, DEPTH), 1)
    same_case = row_case == ((col >> 2) & 1)
    first_part = jnp.zeros((BIG, DEPTH), jnp.bool_)
    for g, (part, _) in enumerate(GROUPS):
        if part == 0:
            first_part = first_part | ((col >> 6) == g)

    def split_matrix(matrix):
        mat_ref[...] = jnp.where(same_case, matrix, 0.0)
        matrix = mat_ref[...]
        head = matrix.astype(jnp.bfloat16).astype(jnp.float32)
        return jnp.where(first_part, head, matrix - head).astype(jnp.bfloat16)

    def expand(left, block, side, right):
        mid_ref[...] = dot(left, block, 1, side)
        return dot(mid_ref[...], right, 1, 1)

    big_d = expand(e_p, coup, 0, w_u)
    big_g = expand(e_u, coup, 1, w_p)
    big_b = expand(e_u, brink, 1, w_u)
    sum_ref[...] = big_d + big_g
    sum_ref[...] += expand(e_u, visc, 1, w_u)
    sum_ref[...] -= expand(e_p, stab, 1, w_p)
    lhs_j[0:BIG] = split_matrix(sum_ref[...])
    lhs_j[BIG : 2 * BIG] = split_matrix(big_b)
    lhs_d[...] = split_matrix(big_d)
    lhs_g[...] = split_matrix(big_g)
    lhs_s[...] = split_matrix(expand(e_s, coup * coup, 0, w_u))

    def diagonal(matrix, hot):
        size = matrix.shape[0]
        eye = lax.broadcasted_iota(jnp.int32, (size, size), 0) == lax.broadcasted_iota(
            jnp.int32, (size, size), 1
        )
        row = jnp.sum(jnp.where(eye, matrix, 0.0), axis=0, keepdims=True)
        column = jnp.sum(hot * row, axis=1, keepdims=True)
        return jnp.broadcast_to(column, (BIG, LANES))

    def node_rows(element_out, target):
        near = [None] * ROWS
        far = [None] * ROWS

        def put(store, at, value):
            store[at] = value if store[at] is None else store[at] + value

        for a in range(EX):
            blocks = element_out(a)
            for b in range(EY):
                for q in range(8):
                    at = (a + q // 4) * (EY + 1) + b + q // 2 % 2
                    put(far if q % 2 else near, at, blocks[b][q])
        for r in range(ROWS):
            target[r] = near[r] + pltpu.roll(far[r], 1, 1)

    def split_nodes(source):
        for r in range(ROWS):
            x = source(r)
            rest = jnp.concatenate(
                [
                    jnp.where(inside, x, 0.0),
                    jnp.where(inside, pltpu.roll(x, LANES - 1, 1), 0.0),
                ],
                axis=0,
            )
            for part in range(PARTS):
                head = rest.astype(jnp.bfloat16)
                t_ref[part, r * 16 : (r + 1) * 16] = head
                rest = rest - head.astype(jnp.float32)

    def product(lhs, a):
        columns = []
        for b in range(EY):
            pieces = []
            for _, part in GROUPS:
                for r in (a * (EY + 1) + b, (a + 1) * (EY + 1) + b):
                    pieces.append(t_ref[part, r * 16 : (r + 2) * 16])
            columns.append(jnp.concatenate(pieces, axis=0))
        return jnp.dot(
            lhs[...], jnp.concatenate(columns, axis=1), preferred_element_type=jnp.float32
        )

    def corner(out, b, q, base=0):
        return out[base + q * CH : base + (q + 1) * CH, b * LANES : (b + 1) * LANES]

    def plain(lhs):
        def element_out(a):
            out = product(lhs, a)
            return [[corner(out, b, q) for q in range(8)] for b in range(EY)]

        return element_out

    def adjoint(a):
        out = product(lhs_j, a)
        return [
            [
                corner(out, b, q) + brk_ref[a * EY + b] * corner(out, b, q, BIG)
                for q in range(8)
            ]
            for b in range(EY)
        ]

    def diag_out(a):
        return [
            [
                jnp.where(inside, diag_v[q * CH : (q + 1) * CH], 0.0)
                + diag_b[q * CH : (q + 1) * CH] * brk_ref[a * EY + b]
                for q in range(8)
            ]
            for b in range(EY)
        ]

    def copies(e):
        made = []
        for r in range(ROUNDS):
            part = pl.ds(r * IFACE_BLOCKS, IFACE_BLOCKS)
            made.append((part, part, {"sub": partners[r]}))
        base = ROUNDS * IFACE_BLOCKS
        low, high = pl.ds(base, FACE_BLOCKS), pl.ds(base + FACE_BLOCKS, FACE_BLOCKS)
        made.append((low, high, {"slab": below}))
        made.append((high, low, {"slab": above}))
        return [
            pltpu.make_async_remote_copy(
                src_ref=send_buf.at[e, src],
                dst_ref=recv_buf.at[e, dst],
                send_sem=send_sem.at[e, i],
                recv_sem=recv_sem.at[e, i],
                device_id=device,
                device_id_type=MESH,
            )
            for i, (src, dst, device) in enumerate(made)
        ]

    started = []

    def post(e, source):
        los = [lo_ref[k] for k in range(BLOCKS)]
        his = [hi_ref[k] for k in range(BLOCKS)]

        def body(r, found):
            row = source[r]
            return tuple(
                jnp.where(
                    his[k] == r,
                    jnp.take_along_axis(row, los[k], axis=1, mode="promise_in_bounds"),
                    found[k],
                )
                for k in range(BLOCKS)
            )

        zero = jnp.zeros((CH, LANES), jnp.float32)
        found = lax.fori_loop(0, ROWS, body, (zero,) * BLOCKS, unroll=UNROLL)
        for k in range(BLOCKS):
            send_buf[e, k] = found[k]
        for copy in copies(e):
            copy.start()
            started.append(copy)

    def arrive(e):
        for copy in copies(e):
            copy.wait_recv()

    def received(e, r):
        at = inv_block[r]
        lanes = inv_lane[r]
        total = jnp.zeros((CH, LANES), jnp.float32)
        for k in range(BLOCKS):
            value = jnp.take_along_axis(
                recv_buf[e, k], lanes, axis=1, mode="promise_in_bounds"
            )
            total = jnp.where(at == k + 1, value, total)
        return total

    def each_row(body, sums=0):
        zero = jnp.zeros((CH, LANES), jnp.float32)

        def step(r, carry):
            added = body(r)
            return tuple(c + t for c, t in zip(carry, added))

        return lax.fori_loop(0, ROWS, step, (zero,) * sums, unroll=UNROLL)

    def sub_copies(t):
        return [
            pltpu.make_async_remote_copy(
                src_ref=sub_buf.at[t, sub],
                dst_ref=sub_buf.at[t, sub],
                send_sem=sub_send_sem.at[t, d],
                recv_sem=sub_recv_sem.at[t, d],
                device_id={"sub": peer},
                device_id_type=MESH,
            )
            for d, peer in enumerate(sub_peers)
        ]

    def sub_arrivals(t):
        return [
            pltpu.make_async_copy(
                sub_buf.at[t, lax.rem(sub + n_sub - d, n_sub)],
                sub_buf.at[t, lax.rem(sub + n_sub - d, n_sub)],
                sub_recv_sem.at[t, d - 1],
            )
            for d in range(1, n_sub)
        ]

    def slab_copies(t):
        return [
            pltpu.make_async_remote_copy(
                src_ref=slab_buf.at[t, slab],
                dst_ref=slab_buf.at[t, slab],
                send_sem=slab_send_sem.at[t, d],
                recv_sem=slab_recv_sem.at[t, d],
                device_id={"slab": peer},
                device_id_type=MESH,
            )
            for d, peer in enumerate(slab_peers)
        ]

    def slab_arrivals(t):
        return [
            pltpu.make_async_copy(
                slab_buf.at[t, lax.rem(slab + n_slab - d, n_slab)],
                slab_buf.at[t, lax.rem(slab + n_slab - d, n_slab)],
                slab_recv_sem.at[t, d - 1],
            )
            for d in range(1, n_slab)
        ]

    def reduce_start(t, partial_sums):
        message = jnp.zeros((CH, LANES), jnp.float32)
        for i, value in enumerate(partial_sums):
            total = jnp.sum(value, axis=1, keepdims=True)
            message = jnp.where(lane == i, total, message)
        sub_buf[t, sub] = message
        for copy in sub_copies(t):
            copy.start()
            started.append(copy)

    def reduce_middle(t):
        for copy in sub_arrivals(t):
            copy.wait()
        total = sub_buf[t, 0]
        for i in range(1, n_sub):
            total = total + sub_buf[t, i]
        slab_buf[t, slab] = total
        for copy in slab_copies(t):
            copy.start()
            started.append(copy)

    def reduce_end(t, number):
        for copy in slab_arrivals(t):
            copy.wait()
        total = slab_buf[t, 0]
        for i in range(1, n_slab):
            total = total + slab_buf[t, i]
        first = jnp.sum(jnp.where(chan < 4, total, 0.0), axis=0, keepdims=True)
        second = jnp.sum(jnp.where(chan < 4, 0.0, total), axis=0, keepdims=True)
        total = jnp.where(chan < 4, first, second)
        return [
            jnp.broadcast_to(total[:, i : i + 1], (CH, LANES)) for i in range(number)
        ]

    pl.semaphore_wait(barrier, n_sub - 1 + n_slab - 1)

    post(0, y_ref)
    diag_v = diagonal(visc, e_u)
    diag_b = diagonal(brink, e_u)
    node_rows(diag_out, y2_ref)
    post(1, y2_ref)
    arrive(0)

    def load_row(r):
        value = y_ref[r] + received(0, r)
        x_ref[r] = value
        return (value * value * wt_ref[r],)

    (square,) = each_row(load_row, 1)
    products = (square,)
    arrive(1)

    def diag_row(r):
        diag_ref[r] = jnp.where(is_p, 1.0, y2_ref[r] + received(1, r))
        return ()

    each_row(diag_row)

    heights = []
    start_norm = None
    exchange = 2
    for step in range(KRYLOV):
        split_nodes(lambda r: x_ref[r] / diag_ref[r])
        node_rows(plain(lhs_d), y_ref)
        if step == 0:
            diag_s = diagonal(stab, e_s)
            split_nodes(lambda r: 1.0 / diag_ref[r])

            def schur_out(a):
                out = product(lhs_s, a)
                return [
                    [
                        corner(out, b, q)
                        + jnp.where(inside, diag_s[q * CH : (q + 1) * CH], 0.0)
                        for q in range(8)
                    ]
                    for b in range(EY)
                ]

            node_rows(schur_out, y2_ref)
            for r in range(ROWS):
                y_ref[r] = y_ref[r] + y2_ref[r]
        post(exchange, y_ref)
        reduce_start(step, products)
        arrive(exchange)

        def pressure_row(r, step=step, exchange=exchange):
            value = y_ref[r] + received(exchange, r)
            if step == 0:
                schur = jnp.where(is_p, pltpu.roll(value, 3, 0), 1.0)
                schur_ref[r] = schur
            else:
                schur = schur_ref[r]
            p_ref[r] = jnp.where(is_p, (value - x_ref[r]) / schur, 0.0)
            return ()

        each_row(pressure_row)
        split_nodes(lambda r: p_ref[r])
        node_rows(plain(lhs_g), y_ref)
        post(exchange + 1, y_ref)
        reduce_middle(step)
        arrive(exchange + 1)

        sums = reduce_end(step, step + 1)
        if step == 0:
            start_norm = jnp.sqrt(sums[0])
            height, length = [], start_norm
        else:
            height, squared = sums[:step], sums[step]
            length = jnp.sqrt(squared - sum(h * h for h in height))
            heights.append(height + [length])

        def direction_row(r, step=step, exchange=exchange, height=height, length=length):
            x = x_ref[r]
            diag = diag_ref[r]
            value = y_ref[r] + received(exchange + 1, r)
            z = jnp.where(is_p, p_ref[r], x / diag - value / diag)
            for m, h in enumerate(height):
                z = z - h * z_ref[m, r]
                x = x - h * v_ref[m, r]
            z_ref[step, r] = z / length
            v_ref[step, r] = x / length
            return ()

        each_row(direction_row)
        split_nodes(lambda r: z_ref[step, r])
        node_rows(adjoint, y_ref)
        post(exchange + 2, y_ref)
        arrive(exchange + 2)

        def image_row(r, step=step, exchange=exchange):
            w = y_ref[r] + received(exchange + 2, r)
            x_ref[r] = w
            weighted = w * wt_ref[r]
            return tuple(v_ref[m, r] * weighted for m in range(step + 1)) + (w * weighted,)

        products = each_row(image_row, step + 2)
        exchange += 3

    reduce_start(KRYLOV, products)
    reduce_middle(KRYLOV)
    sums = reduce_end(KRYLOV, KRYLOV + 1)
    height, squared = sums[:KRYLOV], sums[KRYLOV]
    heights.append(height + [jnp.sqrt(squared - sum(h * h for h in height))])

    def normal(i, j):
        return sum(heights[i][m] * heights[j][m] for m in range(min(i, j) + 2))

    factor = [[None] * KRYLOV for _ in range(KRYLOV)]
    for i in range(KRYLOV):
        for j in range(i + 1):
            value = normal(i, j)
            for k in range(j):
                value = value - factor[i][k] * factor[j][k]
            factor[i][j] = jnp.sqrt(value) if i == j else value / factor[j][j]
    middle = []
    for i in range(KRYLOV):
        value = start_norm * heights[i][0]
        for k in range(i):
            value = value - factor[i][k] * middle[k]
        middle.append(value / factor[i][i])
    coefs = [None] * KRYLOV
    for i in reversed(range(KRYLOV)):
        value = middle[i]
        for k in range(i + 1, KRYLOV):
            value = value - factor[k][i] * coefs[k]
        coefs[i] = value / factor[i][i]

    table = jnp.zeros((CH, LANES), jnp.float32)
    for j in range(KRYLOV):
        table = jnp.where(lane == j, coefs[j], table)
    for case in range(CASES):
        coef_ref[case : case + 1, :] = table[case * 4 : case * 4 + 1, 0:KRYLOV]
    for r in range(ROWS):
        value = coefs[0] * z_ref[0, r]
        for j in range(1, KRYLOV):
            value = value + coefs[j] * z_ref[j, r]
        cols = slice(r * LANES, (r + 1) * LANES)
        for case in range(CASES):
            out_ref[0, 0, case, :, cols] = value[case * 4 : case * 4 + 4]

    for copy in started:
        copy.wait_send()


def per_device(
    n_sub,
    n_slab,
    adjoint_load,
    design,
    viscous_block,
    brinkman_block,
    coupling,
    stabilization,
    neighbours,
    iface_nodes,
    iface_count,
    face_nodes,
    owner_ids,
):
    tile = (CH, LANES)
    f32, i32, bf16 = jnp.float32, jnp.int32, jnp.bfloat16
    rows = (ROWS,) + tile
    dma = pltpu.SemaphoreType.DMA
    scratch = [
        pltpu.VMEM((BLOCKS,) + tile, i32),
        pltpu.VMEM((BLOCKS,) + tile, i32),
        pltpu.VMEM(rows, i32),
        pltpu.VMEM(rows, i32),
        pltpu.VMEM(rows, f32),
        pltpu.VMEM(rows, f32),
        pltpu.VMEM(rows, f32),
        pltpu.VMEM(rows, f32),
        pltpu.VMEM((PARTS, ROWS * 16, LANES), bf16),
        pltpu.VMEM(rows, f32),
        pltpu.VMEM(rows, f32),
        pltpu.VMEM(rows, f32),
        pltpu.VMEM((KRYLOV,) + rows, f32),
        pltpu.VMEM((KRYLOV,) + rows, f32),
        pltpu.VMEM((CH, EX * EY * LANES), f32),
        pltpu.VMEM((EX * EY,) + tile, f32),
        pltpu.VMEM((2 * BIG, DEPTH), bf16),
        pltpu.VMEM((BIG, DEPTH), bf16),
        pltpu.VMEM((BIG, DEPTH), bf16),
        pltpu.VMEM((BIG, DEPTH), bf16),
        pltpu.VMEM((EXCHANGES, BLOCKS) + tile, f32),
        pltpu.VMEM((EXCHANGES, BLOCKS) + tile, f32),
        pltpu.VMEM((REDUCTIONS, n_sub) + tile, f32),
        pltpu.VMEM((4, LANES, LANES), f32),
        pltpu.VMEM((BIG, LANES), f32),
        pltpu.VMEM((BIG, DEPTH), f32),
        pltpu.VMEM((BIG, DEPTH), f32),
        pltpu.VMEM((REDUCTIONS, n_slab) + tile, f32),
        dma((EXCHANGES, ROUNDS + 2)),
        dma((EXCHANGES, ROUNDS + 2)),
        dma((REDUCTIONS, n_sub - 1)),
        dma((REDUCTIONS, n_sub - 1)),
        dma((REDUCTIONS, n_slab - 1)),
        dma((REDUCTIONS, n_slab - 1)),
        dma((INPUTS,)),
    ]
    vmem = pl.BlockSpec(memory_space=pltpu.VMEM)
    operands = (
        adjoint_load,
        design,
        viscous_block,
        brinkman_block,
        coupling,
        stabilization,
        iface_nodes,
        iface_count,
        face_nodes,
        owner_ids,
    )
    scratch += [pltpu.VMEM(x.shape, x.dtype) for x in operands]
    return pl.pallas_call(
        functools.partial(kernel, n_sub, n_slab),
        out_shape=(
            jax.ShapeDtypeStruct((1, 1, CASES, 4, NODES), f32),
            jax.ShapeDtypeStruct((CASES, KRYLOV), f32),
        ),
        in_specs=[pl.BlockSpec(memory_space=pl.ANY)] * INPUTS,
        out_specs=(vmem, vmem),
        scratch_shapes=scratch,
        compiler_params=pltpu.CompilerParams(
            collective_id=0, has_side_effects=True, vmem_limit_bytes=48 * 1024 * 1024
        ),
    )(*operands)


def solution(mesh):
    placed = (
        P("slab", "sub", None, None, None),
        P("slab", "sub", None),
        P(),
        P(),
        P(),
        P(),
        P("slab", "sub", None),
        P("slab", "sub", None, None),
        P("slab", "sub", None),
        P("slab", "sub", None, None),
        P("slab", "sub", None, None),
    )
    return jax.shard_map(
        functools.partial(per_device, mesh.shape["sub"], mesh.shape["slab"]),
        mesh=mesh,
        in_specs=placed,
        out_specs=(P("slab", "sub", None, None, None), P()),
        check_vma=False,
    )
```

```python
import functools

import jax
import jax.numpy as jnp
from jax import lax
from jax.experimental import pallas as pl
from jax.experimental.pallas import tpu as pltpu
from jax.sharding import PartitionSpec as P

EX = 4
EY = 4
EZ = 127
IFACE = 256
FACE = 512
ROUNDS = 3
KRYLOV = 3
CASES = 2
ELEMS = 2032
NODES = 3200

LANES = 128
ROWS = NODES // LANES
CH = 8
SLOTS = ROUNDS * IFACE + 2 * FACE
BLOCKS = SLOTS // LANES
FACE_BLOCKS = FACE // LANES
IFACE_BLOCKS = IFACE // LANES
BIG = 8 * CH

GROUPS = ((0, 0), (0, 1), (1, 0))
DEPTH = BIG * len(GROUPS)
PARTS = 2

BRINKMAN_MAX = 4.0
RAMP_PARAM = 0.1
EXCHANGES = 2 + 3 * KRYLOV
REDUCTIONS = KRYLOV + 1
UNROLL = ROWS
INPUTS = 10
HIGH = lax.Precision.HIGHEST
MESH = pl.DeviceIdType.MESH


def dot(a, b, ca, cb):
    return lax.dot_general(
        a, b, (((ca,), (cb,)), ((), ())), precision=HIGH, preferred_element_type=jnp.float32
    )


def one_hot(rows, cols, field, per_field):
    i = lax.broadcasted_iota(jnp.int32, (rows, cols), 0) & (BIG - 1)
    j = lax.broadcasted_iota(jnp.int32, (rows, cols), 1)
    same = (i >> 3) == (j & 7)
    f = i & 3
    if per_field:
        match = (f == (j >> 3)) & (j < 24)
    else:
        match = (f == field) & (j < 8)
    return jnp.where(same & match, 1.0, 0.0).astype(jnp.float32)


def kernel(
    n_sub,
    n_slab,
    *refs,
):
    inputs = refs[:INPUTS]
    (
        out_ref,
        coef_ref,
        lo_ref,
        hi_ref,
        inv_block,
        inv_lane,
        wt_ref,
        x_ref,
        y_ref,
        y2_ref,
        t_ref,
        p_ref,
        diag_ref,
        schur_ref,
        z_ref,
        v_ref,
        flat_ref,
        brk_ref,
        lhs_j,
        lhs_d,
        lhs_g,
        lhs_s,
        send_buf,
        recv_buf,
        sub_buf,
        pad_ref,
        mid_ref,
        mat_ref,
        sum_ref,
        slab_buf,
        send_sem,
        recv_sem,
        sub_send_sem,
        sub_recv_sem,
        slab_send_sem,
        slab_recv_sem,
        in_sem,
        *held,
    ) = refs[INPUTS:]
    fetches = [
        pltpu.make_async_copy(source, target, in_sem.at[i])
        for i, (source, target) in enumerate(zip(inputs, held))
    ]
    for fetch in fetches:
        fetch.start()
    (
        load_ref,
        design_ref,
        visc_ref,
        brink_ref,
        coup_ref,
        stab_ref,
        iface_ref,
        count_ref,
        face_ref,
        owner_ref,
    ) = held
    sub = lax.axis_index("sub")
    slab = lax.axis_index("slab")
    sub_peers = [lax.rem(sub + d, n_sub) for d in range(1, n_sub)]
    slab_peers = [lax.rem(slab + d, n_slab) for d in range(1, n_slab)]
    partners = [
        sub + (1 << r) * (1 - 2 * lax.rem(sub // (1 << r), 2)) for r in range(ROUNDS)
    ]
    below = lax.rem(slab + n_slab - 1, n_slab)
    above = lax.rem(slab + 1, n_slab)

    barrier = pltpu.get_barrier_semaphore()
    for peer in sub_peers:
        pl.semaphore_signal(barrier, inc=1, device_id={"sub": peer}, device_id_type=MESH)
    for peer in slab_peers:
        pl.semaphore_signal(barrier, inc=1, device_id={"slab": peer}, device_id_type=MESH)

    for fetch in fetches:
        fetch.wait()

    lane = lax.broadcasted_iota(jnp.int32, (CH, LANES), 1)
    chan = lax.broadcasted_iota(jnp.int32, (CH, LANES), 0)
    is_p = (chan & 3) == 3
    inside = lane < EZ

    idx_parts, used_parts, lost_parts = [], [], []
    counts = count_ref[0]
    for r in range(ROUNDS):
        idx_parts.append(iface_ref[0, 0, r : r + 1, :])
        slot = lax.broadcasted_iota(jnp.int32, (1, IFACE), 1)
        used = slot < counts[:, r : r + 1]
        other = owner_ref[0, 0, r : r + 1, :] != sub
        used_parts.append(jnp.where(used, 1.0, 0.0))
        lost_parts.append(jnp.where(used & other, 1.0, 0.0))
    for side in range(2):
        idx_parts.append(face_ref[0, 0, side : side + 1, :])
        linked = slab > 0 if side == 0 else slab < n_slab - 1
        flag = jnp.where(linked, 1.0, 0.0).astype(jnp.float32)
        used_parts.append(jnp.full((1, FACE), 1.0, jnp.float32) * flag)
        lost_parts.append(
            jnp.full((1, FACE), 1.0 if side == 0 else 0.0, jnp.float32) * flag
        )
    idx = jnp.concatenate(idx_parts, axis=1)
    used = jnp.concatenate(used_parts, axis=1)
    lost = jnp.concatenate(lost_parts, axis=1)
    hi = idx >> 7
    lo = idx & (LANES - 1)
    for k in range(BLOCKS):
        cols = slice(k * LANES, (k + 1) * LANES)
        lo_ref[k] = jnp.broadcast_to(lo[:, cols], (CH, LANES))
        hi_ref[k] = jnp.broadcast_to(hi[:, cols], (CH, LANES))

    slot = lax.broadcasted_iota(jnp.int32, (1, SLOTS), 1)
    block_of = ((slot >> 7) + 1).astype(jnp.float32) * used
    lane_of = (slot & (LANES - 1)).astype(jnp.float32) * used
    hot_hi = lax.broadcasted_iota(jnp.int32, (32, SLOTS), 0) == hi
    hot_lo = jnp.where(
        lax.broadcasted_iota(jnp.int32, (LANES, SLOTS), 0) == lo, 1.0, 0.0
    ).astype(jnp.bfloat16)

    def to_nodes(values):
        left = jnp.where(hot_hi, values, 0.0).astype(jnp.bfloat16)
        return lax.dot_general(
            left, hot_lo, (((1,), (1,)), ((), ())), preferred_element_type=jnp.float32
        )

    node_block = to_nodes(block_of).astype(jnp.int32)
    node_lane = to_nodes(lane_of).astype(jnp.int32)
    node_lost = to_nodes(lost)
    for r in range(ROWS):
        inv_block[r] = jnp.broadcast_to(node_block[r : r + 1], (CH, LANES))
        inv_lane[r] = jnp.broadcast_to(node_lane[r : r + 1], (CH, LANES))
        wt_ref[r] = jnp.broadcast_to(1.0 - node_lost[r : r + 1], (CH, LANES))

    for r in range(ROWS):
        cols = slice(r * LANES, (r + 1) * LANES)
        both = jnp.concatenate([load_ref[0, 0, 0, :, cols], load_ref[0, 0, 1, :, cols]], axis=0)
        y_ref[r] = both * wt_ref[r]

    flat_ref[...] = jnp.zeros_like(flat_ref)
    flat_ref[:, 0:ELEMS] = jnp.broadcast_to(design_ref[0], (CH, ELEMS))
    for i in range(EX * EY):
        here = flat_ref[:, i * LANES : (i + 1) * LANES]
        if i > 0:
            before = flat_ref[:, (i - 1) * LANES : i * LANES]
            here = jnp.where(lane < i, pltpu.roll(before, i, 1), pltpu.roll(here, i, 1))
        value = BRINKMAN_MAX * RAMP_PARAM * (1.0 - here) / (RAMP_PARAM + here)
        brk_ref[i] = jnp.where(inside, value, 0.0)

    pad_ref[...] = jnp.zeros_like(pad_ref)
    for i, block in enumerate((visc_ref, brink_ref, coup_ref, stab_ref)):
        pad_ref[i, 0 : block.shape[0], 0 : block.shape[1]] = block[...]
    visc, brink, coup, stab = (pad_ref[i] for i in range(4))
    e_u = one_hot(BIG, LANES, 0, True)
    e_p = one_hot(BIG, LANES, 3, False)
    e_s = one_hot(BIG, LANES, 0, False)
    w_u = one_hot(DEPTH, LANES, 0, True)
    w_p = one_hot(DEPTH, LANES, 3, False)
    row_case = (lax.broadcasted_iota(jnp.int32, (BIG, DEPTH), 0) >> 2) & 1
    col = lax.broadcasted_iota(jnp.int32, (BIG, DEPTH), 1)
    same_case = row_case == ((col >> 2) & 1)
    first_part = jnp.zeros((BIG, DEPTH), jnp.bool_)
    for g, (part, _) in enumerate(GROUPS):
        if part == 0:
            first_part = first_part | ((col >> 6) == g)

    def split_matrix(matrix):
        mat_ref[...] = jnp.where(same_case, matrix, 0.0)
        matrix = mat_ref[...]
        head = matrix.astype(jnp.bfloat16).astype(jnp.float32)
        return jnp.where(first_part, head, matrix - head).astype(jnp.bfloat16)

    def expand(left, block, side, right):
        mid_ref[...] = dot(left, block, 1, side)
        return dot(mid_ref[...], right, 1, 1)

    big_d = expand(e_p, coup, 0, w_u)
    big_g = expand(e_u, coup, 1, w_p)
    big_b = expand(e_u, brink, 1, w_u)
    sum_ref[...] = big_d + big_g
    sum_ref[...] += expand(e_u, visc, 1, w_u)
    sum_ref[...] -= expand(e_p, stab, 1, w_p)
    lhs_j[0:BIG] = split_matrix(sum_ref[...])
    lhs_j[BIG : 2 * BIG] = split_matrix(big_b)
    lhs_d[...] = split_matrix(big_d)
    lhs_g[...] = split_matrix(big_g)
    lhs_s[...] = split_matrix(expand(e_s, coup * coup, 0, w_u))

    def diagonal(matrix, hot):
        size = matrix.shape[0]
        eye = lax.broadcasted_iota(jnp.int32, (size, size), 0) == lax.broadcasted_iota(
            jnp.int32, (size, size), 1
        )
        row = jnp.sum(jnp.where(eye, matrix, 0.0), axis=0, keepdims=True)
        column = jnp.sum(hot * row, axis=1, keepdims=True)
        return jnp.broadcast_to(column, (BIG, LANES))

    def node_rows(element_out, target):
        near = [None] * ROWS
        far = [None] * ROWS

        def put(store, at, value):
            store[at] = value if store[at] is None else store[at] + value

        for a in range(EX):
            blocks = element_out(a)
            for b in range(EY):
                for q in range(8):
                    at = (a + q // 4) * (EY + 1) + b + q // 2 % 2
                    put(far if q % 2 else near, at, blocks[b][q])
        for r in range(ROWS):
            target[r] = near[r] + pltpu.roll(far[r], 1, 1)

    def split_nodes(source):
        for r in range(ROWS):
            x = source(r)
            rest = jnp.concatenate(
                [
                    jnp.where(inside, x, 0.0),
                    jnp.where(inside, pltpu.roll(x, LANES - 1, 1), 0.0),
                ],
                axis=0,
            )
            for part in range(PARTS):
                head = rest.astype(jnp.bfloat16)
                t_ref[part, r * 16 : (r + 1) * 16] = head
                rest = rest - head.astype(jnp.float32)

    def product(lhs, a):
        columns = []
        for b in range(EY):
            pieces = []
            for _, part in GROUPS:
                for r in (a * (EY + 1) + b, (a + 1) * (EY + 1) + b):
                    pieces.append(t_ref[part, r * 16 : (r + 2) * 16])
            columns.append(jnp.concatenate(pieces, axis=0))
        return jnp.dot(
            lhs[...], jnp.concatenate(columns, axis=1), preferred_element_type=jnp.float32
        )

    def corner(out, b, q, base=0):
        return out[base + q * CH : base + (q + 1) * CH, b * LANES : (b + 1) * LANES]

    def plain(lhs):
        def element_out(a):
            out = product(lhs, a)
            return [[corner(out, b, q) for q in range(8)] for b in range(EY)]

        return element_out

    def adjoint(a):
        out = product(lhs_j, a)
        return [
            [
                corner(out, b, q) + brk_ref[a * EY + b] * corner(out, b, q, BIG)
                for q in range(8)
            ]
            for b in range(EY)
        ]

    def diag_out(a):
        return [
            [
                jnp.where(inside, diag_v[q * CH : (q + 1) * CH], 0.0)
                + diag_b[q * CH : (q + 1) * CH] * brk_ref[a * EY + b]
                for q in range(8)
            ]
            for b in range(EY)
        ]

    def copies(e):
        made = []
        for r in range(ROUNDS):
            part = pl.ds(r * IFACE_BLOCKS, IFACE_BLOCKS)
            made.append((part, part, {"sub": partners[r]}))
        base = ROUNDS * IFACE_BLOCKS
        low, high = pl.ds(base, FACE_BLOCKS), pl.ds(base + FACE_BLOCKS, FACE_BLOCKS)
        made.append((low, high, {"slab": below}))
        made.append((high, low, {"slab": above}))
        return [
            pltpu.make_async_remote_copy(
                src_ref=send_buf.at[e, src],
                dst_ref=recv_buf.at[e, dst],
                send_sem=send_sem.at[e, i],
                recv_sem=recv_sem.at[e, i],
                device_id=device,
                device_id_type=MESH,
            )
            for i, (src, dst, device) in enumerate(made)
        ]

    started = []

    def post(e, source):
        los = [lo_ref[k] for k in range(BLOCKS)]
        his = [hi_ref[k] for k in range(BLOCKS)]

        def body(r, found):
            row = source[r]
            return tuple(
                jnp.where(
                    his[k] == r,
                    jnp.take_along_axis(row, los[k], axis=1, mode="promise_in_bounds"),
                    found[k],
                )
                for k in range(BLOCKS)
            )

        zero = jnp.zeros((CH, LANES), jnp.float32)
        found = lax.fori_loop(0, ROWS, body, (zero,) * BLOCKS, unroll=UNROLL)
        for k in range(BLOCKS):
            send_buf[e, k] = found[k]
        for copy in copies(e):
            copy.start()
            started.append(copy)

    def arrive(e):
        for copy in copies(e):
            copy.wait_recv()

    def received(e, r):
        at = inv_block[r]
        lanes = inv_lane[r]
        total = jnp.zeros((CH, LANES), jnp.float32)
        for k in range(BLOCKS):
            value = jnp.take_along_axis(
                recv_buf[e, k], lanes, axis=1, mode="promise_in_bounds"
            )
            total = jnp.where(at == k + 1, value, total)
        return total

    def each_row(body, sums=0):
        zero = jnp.zeros((CH, LANES), jnp.float32)

        def step(r, carry):
            added = body(r)
            return tuple(c + t for c, t in zip(carry, added))

        return lax.fori_loop(0, ROWS, step, (zero,) * sums, unroll=UNROLL)

    def sub_copies(t):
        return [
            pltpu.make_async_remote_copy(
                src_ref=sub_buf.at[t, sub],
                dst_ref=sub_buf.at[t, sub],
                send_sem=sub_send_sem.at[t, d],
                recv_sem=sub_recv_sem.at[t, d],
                device_id={"sub": peer},
                device_id_type=MESH,
            )
            for d, peer in enumerate(sub_peers)
        ]

    def sub_arrivals(t):
        return [
            pltpu.make_async_copy(
                sub_buf.at[t, lax.rem(sub + n_sub - d, n_sub)],
                sub_buf.at[t, lax.rem(sub + n_sub - d, n_sub)],
                sub_recv_sem.at[t, d - 1],
            )
            for d in range(1, n_sub)
        ]

    def slab_copies(t):
        return [
            pltpu.make_async_remote_copy(
                src_ref=slab_buf.at[t, slab],
                dst_ref=slab_buf.at[t, slab],
                send_sem=slab_send_sem.at[t, d],
                recv_sem=slab_recv_sem.at[t, d],
                device_id={"slab": peer},
                device_id_type=MESH,
            )
            for d, peer in enumerate(slab_peers)
        ]

    def slab_arrivals(t):
        return [
            pltpu.make_async_copy(
                slab_buf.at[t, lax.rem(slab + n_slab - d, n_slab)],
                slab_buf.at[t, lax.rem(slab + n_slab - d, n_slab)],
                slab_recv_sem.at[t, d - 1],
            )
            for d in range(1, n_slab)
        ]

    def reduce_start(t, partial_sums):
        message = jnp.zeros((CH, LANES), jnp.float32)
        for i, value in enumerate(partial_sums):
            total = jnp.sum(value, axis=1, keepdims=True)
            message = jnp.where(lane == i, total, message)
        sub_buf[t, sub] = message
        for copy in sub_copies(t):
            copy.start()
            started.append(copy)

    def reduce_middle(t):
        for copy in sub_arrivals(t):
            copy.wait()
        total = sub_buf[t, 0]
        for i in range(1, n_sub):
            total = total + sub_buf[t, i]
        slab_buf[t, slab] = total
        for copy in slab_copies(t):
            copy.start()
            started.append(copy)

    def reduce_end(t, number):
        for copy in slab_arrivals(t):
            copy.wait()
        total = slab_buf[t, 0]
        for i in range(1, n_slab):
            total = total + slab_buf[t, i]
        first = jnp.sum(jnp.where(chan < 4, total, 0.0), axis=0, keepdims=True)
        second = jnp.sum(jnp.where(chan < 4, 0.0, total), axis=0, keepdims=True)
        total = jnp.where(chan < 4, first, second)
        return [
            jnp.broadcast_to(total[:, i : i + 1], (CH, LANES)) for i in range(number)
        ]

    pl.semaphore_wait(barrier, n_sub - 1 + n_slab - 1)

    post(0, y_ref)
    diag_v = diagonal(visc, e_u)
    diag_b = diagonal(brink, e_u)
    node_rows(diag_out, y2_ref)
    post(1, y2_ref)
    arrive(0)

    def load_row(r):
        value = y_ref[r] + received(0, r)
        x_ref[r] = value
        return (value * value * wt_ref[r],)

    (square,) = each_row(load_row, 1)
    products = (square,)
    arrive(1)

    def diag_row(r):
        diag_ref[r] = jnp.where(is_p, 1.0, y2_ref[r] + received(1, r))
        return ()

    each_row(diag_row)

    heights = []
    start_norm = None
    exchange = 2
    for step in range(KRYLOV):
        split_nodes(lambda r: x_ref[r] / diag_ref[r])
        node_rows(plain(lhs_d), y_ref)
        if step == 0:
            diag_s = diagonal(stab, e_s)
            split_nodes(lambda r: 1.0 / diag_ref[r])

            def schur_out(a):
                out = product(lhs_s, a)
                return [
                    [
                        corner(out, b, q)
                        + jnp.where(inside, diag_s[q * CH : (q + 1) * CH], 0.0)
                        for q in range(8)
                    ]
                    for b in range(EY)
                ]

            node_rows(schur_out, y2_ref)
            for r in range(ROWS):
                y_ref[r] = y_ref[r] + y2_ref[r]
        post(exchange, y_ref)
        reduce_start(step, products)
        arrive(exchange)

        def pressure_row(r, step=step, exchange=exchange):
            value = y_ref[r] + received(exchange, r)
            if step == 0:
                schur = jnp.where(is_p, pltpu.roll(value, 3, 0), 1.0)
                schur_ref[r] = schur
            else:
                schur = schur_ref[r]
            p_ref[r] = jnp.where(is_p, (value - x_ref[r]) / schur, 0.0)
            return ()

        each_row(pressure_row)
        split_nodes(lambda r: p_ref[r])
        node_rows(plain(lhs_g), y_ref)
        post(exchange + 1, y_ref)
        reduce_middle(step)
        arrive(exchange + 1)

        sums = reduce_end(step, step + 1)
        if step == 0:
            start_norm = jnp.sqrt(sums[0])
            height, length = [], start_norm
        else:
            height, squared = sums[:step], sums[step]
            length = jnp.sqrt(squared - sum(h * h for h in height))
            heights.append(height + [length])

        def direction_row(r, step=step, exchange=exchange, height=height, length=length):
            x = x_ref[r]
            diag = diag_ref[r]
            value = y_ref[r] + received(exchange + 1, r)
            z = jnp.where(is_p, p_ref[r], x / diag - value / diag)
            for m, h in enumerate(height):
                z = z - h * z_ref[m, r]
                x = x - h * v_ref[m, r]
            z_ref[step, r] = z / length
            v_ref[step, r] = x / length
            return ()

        each_row(direction_row)
        split_nodes(lambda r: z_ref[step, r])
        node_rows(adjoint, y_ref)
        post(exchange + 2, y_ref)
        arrive(exchange + 2)

        def image_row(r, step=step, exchange=exchange):
            w = y_ref[r] + received(exchange + 2, r)
            x_ref[r] = w
            weighted = w * wt_ref[r]
            return tuple(v_ref[m, r] * weighted for m in range(step + 1)) + (w * weighted,)

        products = each_row(image_row, step + 2)
        exchange += 3

    reduce_start(KRYLOV, products)
    reduce_middle(KRYLOV)
    sums = reduce_end(KRYLOV, KRYLOV + 1)
    height, squared = sums[:KRYLOV], sums[KRYLOV]
    heights.append(height + [jnp.sqrt(squared - sum(h * h for h in height))])

    def normal(i, j):
        return sum(heights[i][m] * heights[j][m] for m in range(min(i, j) + 2))

    factor = [[None] * KRYLOV for _ in range(KRYLOV)]
    for i in range(KRYLOV):
        for j in range(i + 1):
            value = normal(i, j)
            for k in range(j):
                value = value - factor[i][k] * factor[j][k]
            factor[i][j] = jnp.sqrt(value) if i == j else value / factor[j][j]
    middle = []
    for i in range(KRYLOV):
        value = start_norm * heights[i][0]
        for k in range(i):
            value = value - factor[i][k] * middle[k]
        middle.append(value / factor[i][i])
    coefs = [None] * KRYLOV
    for i in reversed(range(KRYLOV)):
        value = middle[i]
        for k in range(i + 1, KRYLOV):
            value = value - factor[k][i] * coefs[k]
        coefs[i] = value / factor[i][i]

    table = jnp.zeros((CH, LANES), jnp.float32)
    for j in range(KRYLOV):
        table = jnp.where(lane == j, coefs[j], table)
    for case in range(CASES):
        coef_ref[case : case + 1, :] = table[case * 4 : case * 4 + 1, 0:KRYLOV]
    for r in range(ROWS):
        value = coefs[0] * z_ref[0, r]
        for j in range(1, KRYLOV):
            value = value + coefs[j] * z_ref[j, r]
        cols = slice(r * LANES, (r + 1) * LANES)
        for case in range(CASES):
            out_ref[0, 0, case, :, cols] = value[case * 4 : case * 4 + 4]

    for copy in started:
        copy.wait_send()


def per_device(
    n_sub,
    n_slab,
    adjoint_load,
    design,
    viscous_block,
    brinkman_block,
    coupling,
    stabilization,
    neighbours,
    iface_nodes,
    iface_count,
    face_nodes,
    owner_ids,
):
    tile = (CH, LANES)
    f32, i32, bf16 = jnp.float32, jnp.int32, jnp.bfloat16
    rows = (ROWS,) + tile
    dma = pltpu.SemaphoreType.DMA
    scratch = [
        pltpu.VMEM((BLOCKS,) + tile, i32),
        pltpu.VMEM((BLOCKS,) + tile, i32),
        pltpu.VMEM(rows, i32),
        pltpu.VMEM(rows, i32),
        pltpu.VMEM(rows, f32),
        pltpu.VMEM(rows, f32),
        pltpu.VMEM(rows, f32),
        pltpu.VMEM(rows, f32),
        pltpu.VMEM((PARTS, ROWS * 16, LANES), bf16),
        pltpu.VMEM(rows, f32),
        pltpu.VMEM(rows, f32),
        pltpu.VMEM(rows, f32),
        pltpu.VMEM((KRYLOV,) + rows, f32),
        pltpu.VMEM((KRYLOV,) + rows, f32),
        pltpu.VMEM((CH, EX * EY * LANES), f32),
        pltpu.VMEM((EX * EY,) + tile, f32),
        pltpu.VMEM((2 * BIG, DEPTH), bf16),
        pltpu.VMEM((BIG, DEPTH), bf16),
        pltpu.VMEM((BIG, DEPTH), bf16),
        pltpu.VMEM((BIG, DEPTH), bf16),
        pltpu.VMEM((EXCHANGES, BLOCKS) + tile, f32),
        pltpu.VMEM((EXCHANGES, BLOCKS) + tile, f32),
        pltpu.VMEM((REDUCTIONS, n_sub) + tile, f32),
        pltpu.VMEM((4, LANES, LANES), f32),
        pltpu.VMEM((BIG, LANES), f32),
        pltpu.VMEM((BIG, DEPTH), f32),
        pltpu.VMEM((BIG, DEPTH), f32),
        pltpu.VMEM((REDUCTIONS, n_slab) + tile, f32),
        dma((EXCHANGES, ROUNDS + 2)),
        dma((EXCHANGES, ROUNDS + 2)),
        dma((REDUCTIONS, n_sub - 1)),
        dma((REDUCTIONS, n_sub - 1)),
        dma((REDUCTIONS, n_slab - 1)),
        dma((REDUCTIONS, n_slab - 1)),
        dma((INPUTS,)),
    ]
    vmem = pl.BlockSpec(memory_space=pltpu.VMEM)
    operands = (
        adjoint_load,
        design,
        viscous_block,
        brinkman_block,
        coupling,
        stabilization,
        iface_nodes,
        iface_count,
        face_nodes,
        owner_ids,
    )
    scratch += [pltpu.VMEM(x.shape, x.dtype) for x in operands]
    return pl.pallas_call(
        functools.partial(kernel, n_sub, n_slab),
        out_shape=(
            jax.ShapeDtypeStruct((1, 1, CASES, 4, NODES), f32),
            jax.ShapeDtypeStruct((CASES, KRYLOV), f32),
        ),
        in_specs=[pl.BlockSpec(memory_space=pltpu.HBM)] * INPUTS,
        out_specs=(vmem, vmem),
        scratch_shapes=scratch,
        compiler_params=pltpu.CompilerParams(
            collective_id=0, has_side_effects=True, vmem_limit_bytes=48 * 1024 * 1024
        ),
    )(*operands)


def solution(mesh):
    placed = (
        P("slab", "sub", None, None, None),
        P("slab", "sub", None),
        P(),
        P(),
        P(),
        P(),
        P("slab", "sub", None),
        P("slab", "sub", None, None),
        P("slab", "sub", None),
        P("slab", "sub", None, None),
        P("slab", "sub", None, None),
    )
    return jax.shard_map(
        functools.partial(per_device, mesh.shape["sub"], mesh.shape["slab"]),
        mesh=mesh,
        in_specs=placed,
        out_specs=(P("slab", "sub", None, None, None), P()),
        check_vma=False,
    )
```
